32 devices in a mesh: row: 4 (over y, x), col: 8 (over z, core).
Axes of the slice: x: 2, y: 2, z: 4, core: 2. Of those that a mesh axis runs over, the one named last changes fastest.
Arguments:
- panel_outer: bfloat16 [4, 512, 32], P('row', 'col'), may hold values from -6 to 6
- panel_inner: bfloat16 [4, 512, 32], P('row', 'col'), may hold values from -6 to 6
- upper_inner: bfloat16 [96, 512, 32], P('col', 'row'), may hold values from -0.046875 to 0.046875
- upper_outer: bfloat16 [96, 512, 32], P('col', 'row'), may hold values from -0.75 to 0.75
- tile_left: bfloat16 [4, 96, 512, 32], P('row', 'col'), may hold values from -6 to 6
- tile_right: bfloat16 [4, 96, 512, 32], P('row', 'col'), may hold values from -0.75 to 0.75
- dense_rows: bfloat16 [4, 96, 512, 512], P('row', 'col'), may hold values from -6 to 6
- tile_mask: int32 [4, 96], P('row', 'col'), may hold values 0 or 1
- start_block: float32 [64, 32], replicated, may hold values from -6 to 6
Outputs:
- updated: bfloat16 [4, 96, 512, 512], P('row', 'col')
The draws below stay inside these ranges and needn't reach their ends.
Inputs may be any that keep to these rules, and one draw needn't show every extreme that they name: `tile_mask`: 1 marks a low-rank trailing tile, 0 a dense one.
All inputs are finite; a program needn't handle non-finite values. No bound on the sum of `tile_mask` on one device may be relied on, other than what follows from the above.
Results may differ from the reference program's by a relative error of at most 0.0039.
Values may be sent and summed in bfloat16 or wider, within the bound.
No kernel may reach another device: no remote copies, remote signals or barrier semaphores. Data moves between devices by JAX's collectives and lax.ppermute only.
A program may use at most 128 MiB of HBM per device.

```python
import jax
import jax.numpy as jnp
from jax import lax

TILE = 512
RANK = 32
ITERS = 3
NTI = 4
NTJ = 96


def plant(result, key, smallest, largest):
    longest = result.shape.index(max(result.shape))
    spots = []
    for shift in (0, 1):
        where = [jax.random.randint(jax.random.fold_in(key, axis), (), 0, length) for axis, length in enumerate(result.shape)]
        where[longest] = (where[longest] + shift) % result.shape[longest]
        spots.append(tuple(where))
    return result.at[spots[0]].set(smallest).at[spots[1]].set(largest)


def levels(rng, extent, split, smallest, largest):
    gain = 1.0
    for dim, parts in split:
        steps = jax.random.uniform(jax.random.fold_in(jax.random.fold_in(rng, 6), dim), (parts,), jnp.float32, smallest / len(split), largest / len(split))
        gain = gain * jnp.repeat(jnp.exp(steps), extent[dim] // parts).reshape((-1,) + (1,) * (len(extent) - 1 - dim))
    return gain


def noise(own_key, shape, spread, most, cuts=(), kind=jnp.bfloat16):
    gain = levels(own_key, shape, cuts, -0.22, 0.18) if cuts else 1.0
    result = jax.random.normal(own_key, shape, jnp.float32) * spread * gain
    return jnp.minimum(jnp.maximum(result, -most), most).astype(kind)


def setup_inputs(seed: int = 0) -> dict:
    key_of = jax.random.split(jax.random.key(seed), 10)
    panel_outer = noise(key_of[0], (NTI, TILE, RANK), 1.0, 6.0, ((0, 4), (1, 8)))
    panel_inner = noise(key_of[1], (NTI, TILE, RANK), 1.0, 6.0, ((0, 4), (1, 8)))
    upper_inner = noise(key_of[2], (NTJ, TILE, RANK), (TILE * RANK) ** -0.5, 0.046875, ((0, 8), (1, 4)))
    upper_outer = noise(key_of[3], (NTJ, TILE, RANK), (2 * RANK) ** -0.5, 0.75, ((0, 8), (1, 4)))
    tile_left = noise(key_of[4], (NTI, NTJ, TILE, RANK), 1.0, 6.0, ((0, 4), (1, 8)))
    tile_right = noise(key_of[5], (NTI, NTJ, TILE, RANK), (2 * RANK) ** -0.5, 0.75, ((0, 4), (1, 8)))
    dense_rows = noise(key_of[6], (NTI, NTJ, TILE, TILE), 1.0, 6.0, ((0, 4), (1, 8)))
    tile_mask = plant((jax.random.randint(key_of[7], (NTI, NTJ), 0, 2) < 1).astype(jnp.int32), jax.random.fold_in(key_of[7], 1), 0, 1)
    start_block = noise(key_of[8], (2 * RANK, RANK), 1.0, 6.0, (), jnp.float32)
    return {"panel_outer": panel_outer, "panel_inner": panel_inner, "upper_inner": upper_inner, "upper_outer": upper_outer, "tile_left": tile_left, "tile_right": tile_right, "dense_rows": dense_rows, "tile_mask": tile_mask, "start_block": start_block}


HIGHEST_PRECISION = lax.Precision.HIGHEST

def orthonormalize(basis):
    gram_basis = jnp.einsum('jna,jnb->jab', basis, basis, precision=HIGHEST_PRECISION)
    factor = jnp.linalg.cholesky(gram_basis)
    solved = jax.scipy.linalg.solve_triangular(factor, jnp.swapaxes(basis, -1, -2), lower=True)
    return jnp.swapaxes(solved, -1, -2)

def reference(panel_outer, panel_inner, upper_inner, upper_outer, tile_left, tile_right, dense_rows, tile_mask, start_block):
    inner_all = upper_inner.astype(jnp.float32)
    outer_all = upper_outer.astype(jnp.float32)
    identity = jnp.eye(2 * RANK, dtype=jnp.float32)

    def one_row(operands):
        outer, inner, left_tiles, right_tiles, dense, marks = operands
        coupling = jnp.einsum('kr,jks->jrs', inner.astype(jnp.float32), inner_all, precision=HIGHEST_PRECISION)
        product = jnp.einsum('nr,jrs->jns', outer.astype(jnp.float32), coupling, precision=HIGHEST_PRECISION)
        stack = jnp.concatenate([left_tiles.astype(jnp.float32), -product], -1)
        left_gram = jnp.einsum('jna,jnb->jab', stack, stack, precision=HIGHEST_PRECISION) + identity
        factor = jnp.linalg.cholesky(left_gram)
        right = jnp.concatenate([right_tiles.astype(jnp.float32), outer_all], -1)
        right_gram = jnp.einsum('jna,jnb->jab', right, right, precision=HIGHEST_PRECISION) + identity
        kernel = jnp.einsum('jba,jbc,jcd->jad', factor, right_gram, factor, precision=HIGHEST_PRECISION)
        basis = jnp.broadcast_to(start_block, (kernel.shape[0],) + start_block.shape)
        for iteration in range(ITERS):
            basis = orthonormalize(jnp.einsum('jab,jbc->jac', kernel, basis, precision=HIGHEST_PRECISION))
        projector = jnp.einsum('jac,jbc->jab', basis, basis, precision=HIGHEST_PRECISION)
        middle = jnp.einsum('jab,jcb->jac', projector, factor, precision=HIGHEST_PRECISION)
        solved = jax.scipy.linalg.solve_triangular(factor, jnp.swapaxes(stack, -1, -2), lower=True)
        orthonormal = jnp.swapaxes(solved, -1, -2)
        combined = jnp.einsum('jna,jab->jnb', orthonormal, middle, precision=HIGHEST_PRECISION).astype(jnp.bfloat16)
        low = jnp.einsum('jna,jma->jnm', combined.astype(jnp.float32), right, precision=HIGHEST_PRECISION)
        update = (-product).astype(jnp.bfloat16).astype(jnp.float32)
        dense_new = dense.astype(jnp.float32) + jnp.einsum('jna,jma->jnm', update, outer_all, precision=HIGHEST_PRECISION)
        return jnp.where((marks == 1)[:, None, None], low, dense_new).astype(jnp.bfloat16)
    return lax.map(one_row, (panel_outer, panel_inner, tile_left, tile_right, dense_rows, tile_mask))
```

```python
import jax
import jax.numpy as jnp
from jax import lax
from jax.experimental import pallas as pl
from jax.experimental.pallas import tpu as pltpu
from jax.sharding import PartitionSpec as P

ITERS = 3
F32, BF16 = jnp.float32, jnp.bfloat16
HIGHEST = lax.Precision.HIGHEST
SLOTS = 16
GROUPS = 8
NN = (((1,), (0,)), ((), ()))
NT = (((1,), (1,)), ((), ()))
TN = (((0,), (0,)), ((), ()))


def exact(a, b, dims=NN):
    return lax.dot_general(a, b, dims, precision=HIGHEST, preferred_element_type=F32)


def plain(a, b, dims=NN):
    return lax.dot_general(a, b, dims, preferred_element_type=F32)


def split(a):
    high = a.astype(BF16)
    return high, (a - high.astype(F32)).astype(BF16)


def triple(a, b, dims=NN):
    (ah, al), (bh, bl) = split(a), split(b)
    return plain(ah, bh, dims) + (plain(ah, bl, dims) + plain(al, bh, dims))


def inverse_factors(rows_ref, result_ref):
    lane = lax.broadcasted_iota(jnp.int32, (8, 128), 1)
    sub = lax.broadcasted_iota(jnp.int32, (8, 128), 0)
    group, slot = lane // SLOTS, lane % SLOTS
    a = [[None] * 4 for _ in range(4)]
    e = [[None] * 4 for _ in range(4)]
    diag = (sub == group).astype(F32)
    zero = jnp.zeros((8, 128), F32)
    for c in range(4):
        turned = jnp.transpose(rows_ref[c * 128 : (c + 1) * 128, :])
        for jb in range(4):
            a[c][jb] = turned[jb * 8 : (jb + 1) * 8, :]
            e[c][jb] = diag if jb == c else zero
    spread = lambda x, p: jnp.broadcast_to(x[p : p + 1, :], (8, 128))
    for b in range(4):
        r, s = [], []
        for p in range(8):
            index = slot + p * SLOTS
            take = lambda x: jnp.take_along_axis(x, index, axis=1, mode="promise_in_bounds")
            r.append([take(a[b][jb]) if jb >= b else None for jb in range(4)])
            s.append([take(e[b][jb]) if jb < b else ((sub == p).astype(F32) if jb == b else None) for jb in range(4)])
        for p in range(8):
            pivot = spread(r[p][b], p)
            inverse = 1.0 / pivot
            for q in range(p + 1, 8):
                m = spread(r[q][b], p) * inverse
                for jb in range(4):
                    if jb >= b:
                        r[q][jb] = r[q][jb] - m * r[p][jb]
                    if jb <= b:
                        s[q][jb] = s[q][jb] - m * s[p][jb]
            for c in range(b, 4):
                m = spread(a[c][b], p) * inverse
                if c == b:
                    m = jnp.where(group > p, m, 0.0)
                for jb in range(4):
                    if jb >= b:
                        a[c][jb] = a[c][jb] - m * r[p][jb]
                    if jb <= b:
                        e[c][jb] = e[c][jb] - m * s[p][jb]
        pivots = jnp.sum(a[b][b] * diag, axis=0, keepdims=True)
        scale = jnp.broadcast_to(lax.rsqrt(pivots), (8, 128))
        full = jnp.concatenate([e[b][jb] * scale for jb in range(4)], axis=0)
        result_ref[b * 128 : (b + 1) * 128, :] = jnp.transpose(full)


def kernel(
    pos, mask, xy, w0, w1, w2, w3, z0, z1, z2, z3, left, right, start, dense_hbm, out_hbm,
    dense, left_rows, right_rows, turned, gram, right_gram, basis, imaged, coupling, mix, rows, factors, in_sem, out_sem,
):
    tiles, rank, order = left.shape
    r, c = pos[0], pos[1]

    def fetch(t):
        return pltpu.make_async_copy(dense_hbm.at[t], dense.at[t], in_sem.at[t])

    def drain(t):
        return pltpu.make_async_copy(dense.at[t], out_hbm.at[t], out_sem.at[t])

    for t in range(tiles):
        pl.when(mask[t] == 0)(lambda t=t: fetch(t).start())

    lanes = lax.broadcasted_iota(jnp.int32, (rank, 128), 1)
    outer, inner = [], []
    for q in range(4):
        even = xy[c ^ (2 * q)].astype(F32)
        odd = xy[c ^ (2 * q + 1)].astype(F32)
        outer.append(jnp.where(lanes < 64, even, pltpu.roll(odd, 64, 1)).astype(BF16))
        inner.append(jnp.where(lanes < 64, pltpu.roll(even, 64, 1), odd).astype(BF16))
    outer = jnp.concatenate(outer, axis=1)
    inner_all = jnp.concatenate(inner, axis=1)

    for q, (w, z) in enumerate(((w0, z0), (w1, z1), (w2, z2), (w3, z3))):
        at = pl.ds(pl.multiple_of((r ^ q) * 128, 128), 128)
        for t in range(tiles):
            right_rows[t, rank:, at] = z[t]
            turned[t, :rank, at] = w[t]
    identity = (
        lax.broadcasted_iota(jnp.int32, (64, 64), 0) == lax.broadcasted_iota(jnp.int32, (64, 64), 1)
    ).astype(F32)
    panel = plain(outer, outer, NT)
    for t in range(tiles):
        coupling[t] = plain(inner_all, turned[t, :rank, :], NT)
    for t in range(tiles):
        own = left[t]
        left_rows[t, :rank, :] = own
        left_rows[t, rank:, :] = outer
        right_rows[t, :rank, :] = right[t]
        cross = exact(plain(own, outer, NT), coupling[t])
        tail = exact(exact(coupling[t], panel, TN), coupling[t])
        gram[t] = jnp.concatenate(
            [
                jnp.concatenate([plain(own, own, NT), -cross], 1),
                jnp.concatenate([-jnp.transpose(cross), tail], 1),
            ],
            0,
        ) + identity
        right_gram[t] = plain(right_rows[t], right_rows[t], NT) + identity

    def load(t, source):
        return source[pl.ds(t, 32, SLOTS), :]

    def store(t, value):
        rows[pl.ds(t, 32, SLOTS), :] = value

    for t in range(tiles):
        store(t, gram[t, :rank, :rank])
    inverse_factors(rows, factors)
    for t in range(tiles):
        first = exact(load(t, factors), gram[t, :rank, :])
        basis[t] = exact(start[:, :rank], first)
        rest = gram[t, rank:, rank:] - exact(first[:, rank:], first[:, rank:], TN)
        imaged[t, :, :rank] = rest
        store(t, rest)
    inverse_factors(rows, factors)
    for t in range(tiles):
        second = exact(load(t, factors), imaged[t, :, :rank])
        more = exact(start[:, rank:], second)
        imaged[t] = basis[t] + jnp.concatenate([jnp.zeros((rank, rank), F32), more], 1)
    for step in range(ITERS):
        for t in range(tiles):
            moved = triple(imaged[t], right_gram[t])
            image = triple(moved, gram[t])
            basis[t] = moved
            imaged[t] = image
            store(t, exact(image, moved, NT))
        inverse_factors(rows, factors)
        for t in range(tiles):
            imaged[t] = triple(load(t, factors), imaged[t])
            if step == ITERS - 1:
                basis[t] = triple(load(t, factors), basis[t])

    for t in range(tiles):
        top = basis[t]
        tail = triple(top[:, rank:], coupling[t], NT)
        mixed = triple(jnp.concatenate([top[:, :rank], -tail], 1), imaged[t], TN)
        dense_mix = jnp.concatenate(
            [jnp.zeros((rank, 64), F32), jnp.concatenate([jnp.zeros((rank, rank), F32), -coupling[t]], 1)], 0
        )
        mix[t] = jnp.where(mask[t] == 1, mixed, dense_mix)
    for t in range(tiles):
        high, low = split(mix[t])
        combined = (plain(left_rows[t], high, TN) + plain(left_rows[t], low, TN)).astype(BF16)
        result = plain(combined, right_rows[t])

        @pl.when(mask[t] == 0)
        def _():
            fetch(t).wait()
            dense[t] = (result + dense[t].astype(F32)).astype(BF16)

        @pl.when(mask[t] != 0)
        def _():
            dense[t] = result.astype(BF16)

        drain(t).start()
    for t in range(tiles):
        drain(t).wait()


def local_step(pos, mask, xy, ws, zs, left, right, start, dense):
    tiles, rank, order = left.shape
    vmem = pl.BlockSpec(memory_space=pltpu.VMEM)
    smem = pl.BlockSpec(memory_space=pltpu.SMEM)
    hbm = pl.BlockSpec(memory_space=pl.ANY)
    small = pltpu.VMEM((tiles, rank, 2 * rank), F32)
    square = pltpu.VMEM((tiles, 2 * rank, 2 * rank), F32)
    return pl.pallas_call(
        kernel,
        out_shape=jax.ShapeDtypeStruct(dense.shape, BF16),
        in_specs=[smem, smem] + [vmem] * 12 + [hbm],
        out_specs=hbm,
        scratch_shapes=[
            pltpu.VMEM((tiles, order, order), BF16),
            pltpu.VMEM((tiles, 2 * rank, order), BF16),
            pltpu.VMEM((tiles, 2 * rank, order), BF16),
            pltpu.VMEM((tiles, rank, order), BF16),
            square,
            square,
            small,
            small,
            pltpu.VMEM((tiles, rank, rank), F32),
            square,
            pltpu.VMEM((32 * SLOTS, rank), F32),
            pltpu.VMEM((32 * SLOTS, rank), F32),
            pltpu.SemaphoreType.DMA((tiles,)),
            pltpu.SemaphoreType.DMA((tiles,)),
        ],
        compiler_params=pltpu.CompilerParams(vmem_limit_bytes=40 * 1024 * 1024),
    )(pos, mask, xy, *ws, *zs, left, right, start, dense)


def turn(x):
    return jnp.swapaxes(x, -1, -2)


def swap(x, axis, size, step):
    return lax.ppermute(x, axis, [(i, i ^ step) for i in range(size)])


def solution(mesh):
    nrow, ncol = mesh.shape["row"], mesh.shape["col"]

    def shards(
        panel_outer, panel_inner, upper_inner, upper_outer, tile_left, tile_right, dense_rows, tile_mask, start_block
    ):
        pair = jnp.concatenate([turn(panel_outer[0]), turn(panel_inner[0])], -1)
        w, z = turn(upper_inner), turn(upper_outer)
        if nrow == 4 and ncol == 8:
            pos = jnp.stack([lax.axis_index("row"), lax.axis_index("col")]).astype(jnp.int32)
            xy = jnp.stack([pair, swap(pair, "col", 8, 1)])
            ws = [w] + [swap(w, "row", 4, s) for s in (1, 2, 3)]
            zs = [z] + [swap(z, "row", 4, s) for s in (1, 2, 3)]
            xy = jnp.concatenate([xy, swap(xy, "col", 8, 2)])
            xy = jnp.concatenate([xy, swap(xy, "col", 8, 4)])
        else:
            pos = jnp.zeros((2,), jnp.int32)
            both = lax.all_gather(jnp.stack([turn(panel_outer[0]), turn(panel_inner[0])]), "col", axis=2, tiled=True)
            xy = jnp.concatenate([both[0].reshape(32, 8, 64), both[1].reshape(32, 8, 64)], -1).swapaxes(0, 1)
            w = lax.all_gather(w, "row", axis=2, tiled=True)
            z = lax.all_gather(z, "row", axis=2, tiled=True)
            ws = [w[:, :, 128 * q : 128 * q + 128] for q in range(4)]
            zs = [z[:, :, 128 * q : 128 * q + 128] for q in range(4)]
        updated = local_step(
            pos, tile_mask[0], xy, ws, zs, turn(tile_left[0]), turn(tile_right[0]), turn(start_block), dense_rows[0]
        )
        return updated[None]

    placed = (
        P("row", "col", None),
        P("row", "col", None),
        P("col", "row", None),
        P("col", "row", None),
        P("row", "col", None, None),
        P("row", "col", None, None),
        P("row", "col", None, None),
        P("row", "col"),
        P(),
    )
    return jax.shard_map(shards, mesh=mesh, in_specs=placed, out_specs=P("row", "col", None, None), check_vma=False)
```

```python
import jax
import jax.numpy as jnp
from jax import lax
from jax.experimental import pallas as pl
from jax.experimental.pallas import tpu as pltpu
from jax.sharding import PartitionSpec as P

ITERS = 3
F32, BF16 = jnp.float32, jnp.bfloat16
SLOTS = 16
GROUPS = 8
NN = (((1,), (0,)), ((), ()))
NT = (((1,), (1,)), ((), ()))
TN = (((0,), (0,)), ((), ()))


def dot(a, b, dims=NN):
    return lax.dot_general(a, b, dims, preferred_element_type=F32)


def beside(*parts):
    return jnp.concatenate(parts, axis=1)


def below(*parts):
    return jnp.concatenate(parts, axis=0)


def parts2(x):
    high = x.astype(BF16)
    return high, (x - high.astype(F32)).astype(BF16)


def parts3(x):
    high = x.astype(BF16)
    rest = x - high.astype(F32)
    middle = rest.astype(BF16)
    return high, middle, (rest - middle.astype(F32)).astype(BF16)


def pick(lanes_before, x, y):
    lane = lax.broadcasted_iota(jnp.int32, x.shape, 1)
    return jnp.where(lane < lanes_before, x.astype(F32), y.astype(F32)).astype(BF16)


def left_64(x):
    high, low = parts2(x)
    return beside(high, low[:, :64])


def right_64(x):
    high, low = parts2(x)
    return below(high, low, high)


def left_32(x):
    high, middle, low = parts3(x)
    return beside(pick(64, high, middle), pick(32, high, low)[:, :64])


def right_32(x):
    high, middle, low = parts3(x)
    return below(high, middle, high, middle, low, high)


def wide_left(x):
    high, middle, low = parts3(x)
    return beside(high, middle, pick(64, high, low))


def wide_right(x):
    high, middle, low = parts3(x)
    first = pick(64, high, middle)
    return beside(first, first, pick(64, low, high))


def inverse_factors(rows_ref, result_ref, at=0):
    lane = lax.broadcasted_iota(jnp.int32, (8, 128), 1)
    sub = lax.broadcasted_iota(jnp.int32, (8, 128), 0)
    group, slot = lane // SLOTS, lane % SLOTS
    a = [[None] * 4 for _ in range(4)]
    e = [[None] * 4 for _ in range(4)]
    diag = (sub == group).astype(F32)
    zero = jnp.zeros((8, 128), F32)
    for c in range(4):
        turned = jnp.transpose(rows_ref[c * 128 : (c + 1) * 128, :])
        for jb in range(4):
            a[c][jb] = turned[at + jb * 8 : at + (jb + 1) * 8, :]
            e[c][jb] = diag if jb == c else zero
    spread = lambda x, p: jnp.broadcast_to(x[p : p + 1, :], (8, 128))
    for b in range(4):
        r, s = [], []
        for p in range(8):
            index = slot + p * SLOTS
            take = lambda x: jnp.take_along_axis(x, index, axis=1, mode="promise_in_bounds")
            r.append([take(a[b][jb]) if jb >= b else None for jb in range(4)])
            s.append([take(e[b][jb]) if jb < b else ((sub == p).astype(F32) if jb == b else None) for jb in range(4)])
        for p in range(8):
            pivot = spread(r[p][b], p)
            inverse = 1.0 / pivot
            for q in range(p + 1, 8):
                m = spread(r[q][b], p) * inverse
                for jb in range(4):
                    if jb >= b:
                        r[q][jb] = r[q][jb] - m * r[p][jb]
                    if jb <= b:
                        s[q][jb] = s[q][jb] - m * s[p][jb]
            for c in range(b, 4):
                m = spread(a[c][b], p) * inverse
                if c == b:
                    m = jnp.where(group > p, m, 0.0)
                for jb in range(4):
                    if jb >= b:
                        a[c][jb] = a[c][jb] - m * r[p][jb]
                    if jb <= b:
                        e[c][jb] = e[c][jb] - m * s[p][jb]
        pivots = jnp.sum(a[b][b] * diag, axis=0, keepdims=True)
        scale = jnp.broadcast_to(lax.rsqrt(pivots), (8, 128))
        full = below(*[e[b][jb] * scale for jb in range(4)] * 4)
        result_ref[b * 128 : (b + 1) * 128, :] = jnp.transpose(full)


def kernel(
    pos, xy, mask_hbm, start_hbm, wz0, wz1, wz2, wz3, left, right, dense_hbm, out_hbm,
    dense, updated, left_rows, left_columns, right_rows, inner_rows, gram, gram_parts, right_parts, mixer, mixer_parts,
    raw, square, mix_parts, start, basis, imaged, image_parts, wide_rows, rows, factors, mask, load_sem, out_sem,
):
    tiles, rank, order = left.shape
    r, c = pos[0], pos[1]
    every = range(tiles)

    def drain(t):
        return pltpu.make_async_copy(updated.at[t], out_hbm.at[t], out_sem.at[t])

    loads = []
    for q, wz in enumerate((wz0, wz1, wz2, wz3)):
        at = pl.ds(pl.multiple_of((r ^ q) * 128, 128), 128)
        loads.append((wz.at[:, :rank, :], inner_rows.at[:, :, at]))
        loads.append((wz.at[:, rank:, :], right_rows.at[:, rank:, at]))
    loads.append((left, left_rows.at[:, :rank, :]))
    loads.append((right, right_rows.at[:, :rank, :]))
    loads.append((start_hbm, start))
    loads.append((mask_hbm, mask))
    loads.append((dense_hbm, dense))
    loads = [pltpu.make_async_copy(x, y, load_sem.at[i]) for i, (x, y) in enumerate(loads)]
    for copy in loads:
        copy.start()

    lanes = lax.broadcasted_iota(jnp.int32, (rank, 128), 1)
    outer, inner = [], []
    for q in range(4):
        even = xy[c ^ (2 * q)].astype(F32)
        odd = xy[c ^ (2 * q + 1)].astype(F32)
        outer.append(jnp.where(lanes < 64, even, pltpu.roll(odd, 64, 1)).astype(BF16))
        inner.append(jnp.where(lanes < 64, pltpu.roll(even, 64, 1), odd).astype(BF16))
    outer = beside(*outer)
    inner = beside(*inner)
    for t in every:
        left_rows[t, rank:, :] = outer
    for copy in loads[:-1]:
        copy.wait()

    row = lax.broadcasted_iota(jnp.int32, (64, 128), 0)
    lane = lax.broadcasted_iota(jnp.int32, (64, 128), 1)
    identity = (lane % 64 == row).astype(F32)
    tail = lane[:rank] % 64 >= rank

    coupling = dot(inner_rows[...].reshape(tiles * rank, order), below(inner, inner, inner, inner), NT)
    for t in every:
        raw[t] = dot(left_rows[t], below(left_rows[t], left_rows[t]), NT)
    for t in every:
        square[t] = dot(right_rows[t], below(right_rows[t], right_rows[t]), NT) + identity
    for t in every:
        own = -coupling[t * rank : (t + 1) * rank, :]
        mixer[t] = below(identity[:rank], jnp.where(tail, own, 0.0))
        basis[t] = dot(left_32(own), right_32(raw[t, rank:, :]))
    for t in every:
        mixer_parts[t] = right_64(mixer[t])
        right_parts[t] = right_64(square[t])
    for t in every:
        scale = wide_right(mixer[t])
        gram[t] = dot(wide_left(below(raw[t, :rank, :], basis[t])), below(scale, scale), NT) + identity
    for t in every:
        gram_parts[t] = right_64(gram[t])
        wide_rows[pl.ds(t, rank, SLOTS), :] = gram[t, :rank, :]
        left_columns[t] = jnp.transpose(below(left_rows[t], left_rows[t]))

    def inverse(t):
        return factors[pl.ds(t, rank, SLOTS), :]

    head = start[:, :rank]
    head = left_32(beside(head, head, head, head))
    foot = start[:, rank:]
    foot = left_32(beside(foot, foot, foot, foot))
    inverse_factors(wide_rows, factors)
    for t in every:
        basis[t] = dot(left_32(inverse(t)), right_32(gram[t, :rank, :]))
    for t in every:
        mix_parts[t] = right_32(basis[t])
    for t in every:
        first = mix_parts[t]
        high, middle, low = first[:32], first[32:64], first[128:160]
        square[t] = dot(below(high, high, middle, middle, high, low)[:, :64], first, TN)
    for t in every:
        imaged[t] = dot(head, mix_parts[t])
    for t in every:
        basis[t] = jnp.where(tail, gram[t, rank:, :] - square[t, rank:, :], 0.0)
        wide_rows[pl.ds(t, rank, SLOTS), :] = basis[t]
    inverse_factors(wide_rows, factors, rank)
    for t in every:
        basis[t] = dot(left_32(inverse(t)), right_32(basis[t]))
    for t in every:
        imaged[t] = imaged[t] + dot(foot, right_32(basis[t]))
    for step in range(ITERS):
        for t in every:
            basis[t] = dot(left_64(imaged[t]), right_parts[t])
        for t in every:
            imaged[t] = dot(left_64(basis[t]), gram_parts[t])
        for t in every:
            image_parts[t] = below(*parts3(imaged[t]))
            rows[pl.ds(t, rank, SLOTS), :] = dot(wide_left(imaged[t]), wide_right(basis[t]), NT)
        inverse_factors(rows, factors)
        if step < ITERS - 1:
            for t in every:
                imaged[t] = dot(inverse(t).astype(BF16)[:, :96], image_parts[t])
        else:
            for t in every:
                scale = pick(64, *parts2(inverse(t)))
                high, middle = image_parts[t, :32, :], image_parts[t, 32:64, :]
                imaged[t] = dot(scale, below(high, middle, high, middle))
                high, middle = parts2(basis[t])
                basis[t] = dot(scale, below(high, middle, high, middle))

    loads[-1].wait()
    last = (lane[:rank] % 64 == row[:rank] + rank).astype(F32)
    for t in every:
        square[t, :rank, :] = dot(left_64(basis[t]), mixer_parts[t])
    for t in every:
        admissible = mask[0, t] == 1
        high, low = parts2(jnp.where(admissible, square[t, :rank, :], mixer[t, rank:, :])[:, :64])
        raw[t] = dot(below(high, high, low), paired(jnp.where(admissible, imaged[t], last)), TN)
    for t in every:
        mix_parts[t, :128, :] = below(*parts2(raw[t]))

    def combine(t):
        return dot(left_columns[t], mix_parts[t, :128, :64]).astype(BF16)

    combined = combine(0)
    for t in every:
        admissible = mask[0, t] == 1
        following = combine(t + 1) if t + 1 < tiles else None
        for m in range(0, order, 128):
            added = jnp.where(admissible, 0.0, dense[t, m : m + 128, :].astype(F32))
            updated[t, m : m + 128, :] = (dot(combined[m : m + 128, :], right_rows[t]) + added).astype(BF16)
        drain(t).start()
        combined = following
    for t in every:
        drain(t).wait()


def paired(x):
    high, low = parts2(x)
    return below(high, low, high)


def local_step(pos, xy, mask, start, wzs, left, right, dense):
    tiles, rank, order = left.shape
    vmem = pl.BlockSpec(memory_space=pltpu.VMEM)
    smem = pl.BlockSpec(memory_space=pltpu.SMEM)
    hbm = pl.BlockSpec(memory_space=pltpu.HBM)
    free = pl.BlockSpec(memory_space=pl.ANY)
    whole = pltpu.VMEM((tiles, order, order), BF16)
    rows = pltpu.VMEM((tiles, 2 * rank, order), BF16)
    parts = pltpu.VMEM((tiles, 192, 128), BF16)
    square = pltpu.VMEM((tiles, 64, 128), F32)
    small = pltpu.VMEM((tiles, 32, 128), F32)
    return pl.pallas_call(
        kernel,
        out_shape=jax.ShapeDtypeStruct(dense.shape, BF16),
        in_specs=[smem, vmem, hbm, hbm] + [free] * 4 + [hbm] * 3,
        out_specs=hbm,
        scratch_shapes=[
            whole,
            whole,
            rows,
            pltpu.VMEM((tiles, order, 128), BF16),
            rows,
            pltpu.VMEM((tiles, rank, order), BF16),
            square,
            parts,
            parts,
            square,
            parts,
            square,
            square,
            parts,
            pltpu.VMEM((32, 64), F32),
            small,
            small,
            pltpu.VMEM((tiles, 96, 128), BF16),
            pltpu.VMEM((32 * SLOTS, 128), F32),
            pltpu.VMEM((32 * SLOTS, 32), F32),
            pltpu.VMEM((32 * SLOTS, 128), F32),
            pltpu.SMEM((1, tiles), jnp.int32),
            pltpu.SemaphoreType.DMA((13,)),
            pltpu.SemaphoreType.DMA((tiles,)),
        ],
        compiler_params=pltpu.CompilerParams(vmem_limit_bytes=56 * 1024 * 1024),
    )(pos, xy, mask, start, *wzs, left, right, dense)


def turn(x):
    return jnp.swapaxes(x, -1, -2)


def swap(x, axis, size, step):
    return lax.ppermute(x, axis, [(i, i ^ step) for i in range(size)])


def solution(mesh):
    nrow, ncol = mesh.shape["row"], mesh.shape["col"]

    def shards(
        panel_outer, panel_inner, upper_inner, upper_outer, tile_left, tile_right, dense_rows, tile_mask, start_block
    ):
        pair = jnp.concatenate([turn(panel_outer[0]), turn(panel_inner[0])], -1)
        wz = jnp.concatenate([turn(upper_inner), turn(upper_outer)], 1)
        if nrow == 4 and ncol == 8:
            pos = jnp.stack([lax.axis_index("row"), lax.axis_index("col")]).astype(jnp.int32)
            xy = jnp.stack([pair, swap(pair, "col", 8, 1)])
            wzs = [wz] + [swap(wz, "row", 4, s) for s in (1, 2, 3)]
            xy = jnp.concatenate([xy, swap(xy, "col", 8, 2)])
            xy = jnp.concatenate([xy, swap(xy, "col", 8, 4)])
        else:
            pos = jnp.zeros((2,), jnp.int32)
            both = lax.all_gather(jnp.stack([turn(panel_outer[0]), turn(panel_inner[0])]), "col", axis=2, tiled=True)
            xy = jnp.concatenate([both[0].reshape(32, 8, 64), both[1].reshape(32, 8, 64)], -1).swapaxes(0, 1)
            wz = lax.all_gather(wz, "row", axis=2, tiled=True)
            wzs = [wz[:, :, 128 * q : 128 * q + 128] for q in range(4)]
        updated = local_step(
            pos, xy, tile_mask, turn(start_block), wzs, turn(tile_left[0]), turn(tile_right[0]), dense_rows[0]
        )
        return updated[None]

    placed = (
        P("row", "col", None),
        P("row", "col", None),
        P("col", "row", None),
        P("col", "row", None),
        P("row", "col", None, None),
        P("row", "col", None, None),
        P("row", "col", None, None),
        P("row", "col"),
        P(),
    )
    return jax.shard_map(shards, mesh=mesh, in_specs=placed, out_specs=P("row", "col", None, None), check_vma=False)
```

```python
import functools

import jax
import jax.numpy as jnp
from jax import lax
from jax.experimental import pallas as pl
from jax.experimental.pallas import tpu as pltpu
from jax.sharding import PartitionSpec as P

ITERS = 3
F32, BF16 = jnp.float32, jnp.bfloat16
SLOTS = 16
NN = (((1,), (0,)), ((), ()))
NT = (((1,), (1,)), ((), ()))
TN = (((0,), (0,)), ((), ()))


def dot(a, b, dims=NN):
    return lax.dot_general(a, b, dims, preferred_element_type=F32)


def beside(*parts):
    return jnp.concatenate(parts, axis=1)


def below(*parts):
    return jnp.concatenate(parts, axis=0)


def parts2(x):
    high = x.astype(BF16)
    return high, (x - high.astype(F32)).astype(BF16)


def parts3(x):
    high = x.astype(BF16)
    rest = x - high.astype(F32)
    middle = rest.astype(BF16)
    return high, middle, (rest - middle.astype(F32)).astype(BF16)


def pick(lanes_before, x, y):
    lane = lax.broadcasted_iota(jnp.int32, x.shape, 1)
    return jnp.where(lane < lanes_before, x.astype(F32), y.astype(F32)).astype(BF16)


def left_64(x):
    high, low = parts2(x)
    return beside(high, low[:, :64])


def right_64(x):
    high, low = parts2(x)
    return below(high, low, high)


def left_32(x):
    high, middle, low = parts3(x)
    return beside(pick(64, high, middle), pick(32, high, low)[:, :64])


def right_32(x):
    high, middle, low = parts3(x)
    return below(high, middle, high, middle, low, high)


def wide_left(x):
    high, middle, low = parts3(x)
    return beside(high, middle, pick(64, high, low))


def wide_right(x):
    high, middle, low = parts3(x)
    first = pick(64, high, middle)
    return beside(first, first, pick(64, low, high))


def inverse_factors(rows_ref, result_ref, at=0):
    sub = lax.broadcasted_iota(jnp.int32, (8, SLOTS), 0)
    one = [(sub == p).astype(F32) for p in range(8)]
    a = []
    for i in range(32):
        turned = jnp.transpose(rows_ref[i * SLOTS : (i + 1) * SLOTS, :])
        a.append({jb: turned[at + jb * 8 : at + jb * 8 + 8, :] for jb in range(i // 8, 4)})
    e = [{i // 8: one[i % 8]} for i in range(32)]

    def spread(x, p):
        return jnp.broadcast_to(x[p : p + 1, :], (8, SLOTS))

    def less(x, m, y):
        return -(m * y) if x is None else x - m * y

    for b in range(4):
        r, s = a[8 * b : 8 * b + 8], e[8 * b : 8 * b + 8]
        d = [[spread(r[p][b], q) for p in range(q + 1)] for q in range(8)]
        m = [[None] * 8 for _ in range(8)]
        inverse = []
        for p in range(8):
            inverse.append(1.0 / d[p][p])
            for q in range(p + 1, 8):
                m[q][p] = d[q][p] * inverse[p]
                for w in range(p + 1, q + 1):
                    d[q][w] = d[q][w] - m[q][p] * d[w][p]
        for p in range(8):
            for q in range(p + 1, 8):
                for jb in range(b + 1, 4):
                    r[q][jb] = r[q][jb] - m[q][p] * r[p][jb]
                for jb in range(b + 1):
                    s[q][jb] = s[q][jb] - m[q][p] * s[p][jb]
        for c in range(b + 1, 4):
            scaled = [r[p][c] * inverse[p] for p in range(8)]
            for i in range(8 * c, 8 * c + 8):
                for p in range(8):
                    k = spread(scaled[p], i % 8)
                    for jb in range(c, 4):
                        a[i][jb] = a[i][jb] - k * r[p][jb]
                    for jb in range(b + 1):
                        e[i][jb] = less(e[i].get(jb), k, s[p][jb])
        for p in range(8):
            scale = lax.rsqrt(d[p][p])
            full = below(*[s[p][jb] * scale for jb in range(b + 1)], *[jnp.zeros((8, SLOTS), F32)] * (3 - b))
            i = 8 * b + p
            result_ref[i * SLOTS : (i + 1) * SLOTS, :] = jnp.transpose(below(full, full, full, full))


def kernel(
    place, near, far, mask_hbm, start_hbm, wz0, wz1, wz2, wz3, left, right, dense_hbm, out_hbm,
    dense, updated, left_rows, left_columns, right_rows, inner_rows, gram, gram_parts, right_parts, mixer, mixer_parts,
    raw, square, mix_parts, start, basis, imaged, image_parts, wide_rows, rows, factors, mask, load_sem, out_sem,
):
    tiles, rank, order = left.shape
    r, c = place()
    every = range(tiles)

    def drain(t):
        return pltpu.make_async_copy(updated.at[t], out_hbm.at[t], out_sem.at[t])

    loads = []
    for q, wz in enumerate((wz0, wz1, wz2, wz3)):
        at = pl.ds(pl.multiple_of((r ^ q) * 128, 128), 128)
        loads.append((wz.at[:, :rank, :], inner_rows.at[:, :, at]))
        loads.append((wz.at[:, rank:, :], right_rows.at[:, rank:, at]))
    loads.append((left, left_rows.at[:, :rank, :]))
    loads.append((right, right_rows.at[:, :rank, :]))
    loads.append((start_hbm, start))
    loads.append((mask_hbm, mask))
    loads.append((dense_hbm, dense))
    loads = [pltpu.make_async_copy(x, y, load_sem.at[i]) for i, (x, y) in enumerate(loads)]
    for copy in loads:
        copy.start()

    lanes = lax.broadcasted_iota(jnp.int32, (rank, 128), 1)
    outer, inner = [], []
    for q in range(4):
        even, odd = [
            jnp.where((c ^ p) < 4, near[(c ^ p) % 4].astype(F32), far[(c ^ p) % 4].astype(F32)) for p in (2 * q, 2 * q + 1)
        ]
        outer.append(jnp.where(lanes < 64, even, pltpu.roll(odd, 64, 1)).astype(BF16))
        inner.append(jnp.where(lanes < 64, pltpu.roll(even, 64, 1), odd).astype(BF16))
    outer = beside(*outer)
    inner = beside(*inner)
    for t in every:
        left_rows[t, rank:, :] = outer
    for copy in loads[:-1]:
        copy.wait()

    row = lax.broadcasted_iota(jnp.int32, (64, 128), 0)
    lane = lax.broadcasted_iota(jnp.int32, (64, 128), 1)
    identity = (lane % 64 == row).astype(F32)
    tail = lane[:rank] % 64 >= rank

    coupling = dot(inner_rows[...].reshape(tiles * rank, order), below(inner, inner, inner, inner), NT)
    for t in every:
        raw[t] = dot(left_rows[t], below(left_rows[t], left_rows[t]), NT)
    for t in every:
        square[t] = dot(right_rows[t], below(right_rows[t], right_rows[t]), NT) + identity
    for t in every:
        own = -coupling[t * rank : (t + 1) * rank, :]
        mixer[t] = below(identity[:rank], jnp.where(tail, own, 0.0))
        basis[t] = dot(left_32(own), right_32(raw[t, rank:, :]))
    for t in every:
        mixer_parts[t] = right_64(mixer[t])
        right_parts[t] = right_64(square[t])
    for t in every:
        scale = wide_right(mixer[t])
        gram[t] = dot(wide_left(below(raw[t, :rank, :], basis[t])), below(scale, scale), NT) + identity
    for t in every:
        gram_parts[t] = right_64(gram[t])
        wide_rows[pl.ds(t, rank, SLOTS), :] = gram[t, :rank, :]
        left_columns[t] = jnp.transpose(below(left_rows[t], left_rows[t]))

    def inverse(t):
        return factors[pl.ds(t, rank, SLOTS), :]

    head = start[:, :rank]
    head = left_32(beside(head, head, head, head))
    foot = start[:, rank : 2 * rank]
    foot = left_32(beside(foot, foot, foot, foot))
    inverse_factors(wide_rows, factors)
    for t in every:
        basis[t] = dot(left_32(inverse(t)), right_32(gram[t, :rank, :]))
    for t in every:
        mix_parts[t] = right_32(basis[t])
    for t in every:
        first = mix_parts[t]
        high, middle, low = first[:32], first[32:64], first[128:160]
        square[t] = dot(below(high, high, middle, middle, high, low)[:, :64], first, TN)
    for t in every:
        imaged[t] = dot(head, mix_parts[t])
    for t in every:
        basis[t] = jnp.where(tail, gram[t, rank:, :] - square[t, rank:, :], 0.0)
        wide_rows[pl.ds(t, rank, SLOTS), :] = basis[t]
    inverse_factors(wide_rows, factors, rank)
    for t in every:
        basis[t] = dot(left_32(inverse(t)), right_32(basis[t]))
    for t in every:
        imaged[t] = imaged[t] + dot(foot, right_32(basis[t]))
    for step in range(ITERS):
        for t in every:
            basis[t] = dot(left_64(imaged[t]), right_parts[t])
        for t in every:
            imaged[t] = dot(left_64(basis[t]), gram_parts[t])
        for t in every:
            image_parts[t] = below(*parts3(imaged[t]))
            rows[pl.ds(t, rank, SLOTS), :] = dot(wide_left(imaged[t]), wide_right(basis[t]), NT)
        inverse_factors(rows, factors)
        if step < ITERS - 1:
            for t in every:
                imaged[t] = dot(inverse(t).astype(BF16)[:, :96], image_parts[t])
        else:
            for t in every:
                scale = pick(64, *parts2(inverse(t)))
                high, middle = image_parts[t, :32, :], image_parts[t, 32:64, :]
                imaged[t] = dot(scale, below(high, middle, high, middle))
                high, middle = parts2(basis[t])
                basis[t] = dot(scale, below(high, middle, high, middle))

    loads[-1].wait()
    last = (lane[:rank] % 64 == row[:rank] + rank).astype(F32)
    for t in every:
        square[t, :rank, :] = dot(left_64(basis[t]), mixer_parts[t])
    for t in every:
        admissible = mask[0, t] == 1
        high, low = parts2(jnp.where(admissible, square[t, :rank, :], mixer[t, rank:, :])[:, :64])
        raw[t] = dot(below(high, high, low), paired(jnp.where(admissible, imaged[t], last)), TN)
    for t in every:
        mix_parts[t, :128, :] = below(*parts2(raw[t]))

    def combine(t):
        return dot(left_columns[t], mix_parts[t, :128, :64]).astype(BF16)

    combined = combine(0)
    for t in every:
        admissible = mask[0, t] == 1
        following = combine(t + 1) if t + 1 < tiles else None
        for m in range(0, order, 128):
            added = jnp.where(admissible, 0.0, dense[t, m : m + 128, :].astype(F32))
            updated[t, m : m + 128, :] = (dot(combined[m : m + 128, :], right_rows[t]) + added).astype(BF16)
        drain(t).start()
        combined = following
    for t in every:
        drain(t).wait()


def paired(x):
    high, low = parts2(x)
    return below(high, low, high)


def local_step(place, near, far, mask, start, wzs, left, right, dense):
    tiles, rank, order = left.shape
    vmem = pl.BlockSpec(memory_space=pltpu.VMEM)
    hbm = pl.BlockSpec(memory_space=pltpu.HBM)
    free = pl.BlockSpec(memory_space=pl.ANY)
    whole = pltpu.VMEM((tiles, order, order), BF16)
    rows = pltpu.VMEM((tiles, 2 * rank, order), BF16)
    parts = pltpu.VMEM((tiles, 192, 128), BF16)
    square = pltpu.VMEM((tiles, 64, 128), F32)
    small = pltpu.VMEM((tiles, 32, 128), F32)
    return pl.pallas_call(
        functools.partial(kernel, place),
        out_shape=jax.ShapeDtypeStruct(dense.shape, BF16),
        in_specs=[vmem, vmem, free, free] + [free] * 4 + [hbm] * 3,
        out_specs=hbm,
        scratch_shapes=[
            whole,
            whole,
            rows,
            pltpu.VMEM((tiles, order, 128), BF16),
            rows,
            pltpu.VMEM((tiles, rank, order), BF16),
            square,
            parts,
            parts,
            square,
            parts,
            square,
            square,
            parts,
            pltpu.VMEM((32, 128), F32),
            small,
            small,
            pltpu.VMEM((tiles, 96, 128), BF16),
            pltpu.VMEM((32 * SLOTS, 128), F32),
            pltpu.VMEM((32 * SLOTS, 32), F32),
            pltpu.VMEM((32 * SLOTS, 128), F32),
            pltpu.SMEM((1, tiles), jnp.int32),
            pltpu.SemaphoreType.DMA((13,)),
            pltpu.SemaphoreType.DMA((tiles,)),
        ],
        compiler_params=pltpu.CompilerParams(vmem_limit_bytes=53 * 1024 * 1024),
    )(near, far, mask, start, *wzs, left, right, dense)


def turn(x):
    return jnp.swapaxes(x, -1, -2)


def swap(x, axis, size, step):
    return lax.ppermute(x, axis, [(i, i ^ step) for i in range(size)])


def solution(mesh):
    nrow, ncol = mesh.shape["row"], mesh.shape["col"]

    def shards(
        panel_outer, panel_inner, upper_inner, upper_outer, tile_left, tile_right, dense_rows, tile_mask, start_block
    ):
        pair = jnp.concatenate([turn(panel_outer[0]), turn(panel_inner[0])], -1)
        wz = jnp.concatenate([turn(upper_inner), turn(upper_outer)], 1)
        if nrow == 4 and ncol == 8:
            place = lambda: (lax.axis_index("row"), lax.axis_index("col"))
            pair, wz = lax.optimization_barrier((pair, wz))
            near = jnp.stack([pair, swap(pair, "col", 8, 1)])
            wzs = [wz] + [swap(wz, "row", 4, s) for s in (1, 2, 3)]
            near = jnp.concatenate([near, swap(near, "col", 8, 2)])
            far = swap(near, "col", 8, 4)
        else:
            place = lambda: (0, 0)
            both = lax.all_gather(jnp.stack([turn(panel_outer[0]), turn(panel_inner[0])]), "col", axis=2, tiled=True)
            xy = jnp.concatenate([both[0].reshape(32, 8, 64), both[1].reshape(32, 8, 64)], -1).swapaxes(0, 1)
            near, far = xy[:4], xy[4:]
            wz = lax.all_gather(wz, "row", axis=2, tiled=True)
            wzs = [wz[:, :, 128 * q : 128 * q + 128] for q in range(4)]
        flags = (tile_mask == 1).astype(jnp.int32)
        start = jnp.concatenate([turn(start_block), turn(start_block)], 1)
        updated = local_step(
            place, near, far, flags, start, wzs, turn(tile_left[0]), turn(tile_right[0]), dense_rows[0]
        )
        return updated[None]

    placed = (
        P("row", "col", None),
        P("row", "col", None),
        P("col", "row", None),
        P("col", "row", None),
        P("row", "col", None, None),
        P("row", "col", None, None),
        P("row", "col", None, None),
        P("row", "col"),
        P(),
    )
    return jax.shard_map(shards, mesh=mesh, in_specs=placed, out_specs=P("row", "col", None, None), check_vma=False)
```

```python
import functools

import jax
import jax.numpy as jnp
from jax import lax
from jax.experimental import pallas as pl
from jax.experimental.pallas import tpu as pltpu
from jax.sharding import PartitionSpec as P

ITERS = 3
F32, BF16 = jnp.float32, jnp.bfloat16
SLOTS = 16
NN = (((1,), (0,)), ((), ()))
NT = (((1,), (1,)), ((), ()))
TN = (((0,), (0,)), ((), ()))


def dot(a, b, dims=NN):
    return lax.dot_general(a, b, dims, preferred_element_type=F32)


def beside(*parts):
    return jnp.concatenate(parts, axis=1)


def below(*parts):
    return jnp.concatenate(parts, axis=0)


def parts2(x):
    high = x.astype(BF16)
    return high, (x - high.astype(F32)).astype(BF16)


def parts3(x):
    high = x.astype(BF16)
    rest = x - high.astype(F32)
    middle = rest.astype(BF16)
    return high, middle, (rest - middle.astype(F32)).astype(BF16)


def pick(lanes_before, x, y):
    lane = lax.broadcasted_iota(jnp.int32, x.shape, 1)
    return jnp.where(lane < lanes_before, x.astype(F32), y.astype(F32)).astype(BF16)


def left_64(x):
    high, low = parts2(x)
    return beside(high, low[:, :64])


def right_64(x):
    high, low = parts2(x)
    return below(high, low, high)


def left_32(x):
    high, middle, low = parts3(x)
    return beside(pick(64, high, middle), pick(32, high, low)[:, :64])


def right_32(x):
    high, middle, low = parts3(x)
    return below(high, middle, high, middle, low, high)


def wide_left(x):
    high, middle, low = parts3(x)
    return beside(high, middle, pick(64, high, low))


def wide_right(x):
    high, middle, low = parts3(x)
    first = pick(64, high, middle)
    return beside(first, first, pick(64, low, high))


def inverse_factors(rows_ref, result_ref, at=0, beside_it=()):
    sub = lax.broadcasted_iota(jnp.int32, (8, SLOTS), 0)
    one = [(sub == p).astype(F32) for p in range(8)]
    a = []
    for i in range(32):
        turned = jnp.transpose(rows_ref[i * SLOTS : (i + 1) * SLOTS, :])
        a.append({jb: turned[at + jb * 8 : at + jb * 8 + 8, :] for jb in range(i // 8, 4)})
    e = [{i // 8: one[i % 8]} for i in range(32)]

    def spread(x, p):
        return jnp.broadcast_to(x[p : p + 1, :], (8, SLOTS))

    def less(x, m, y):
        return -(m * y) if x is None else x - m * y

    beside_it = list(beside_it)
    for b in range(4):
        for _ in range(-(-len(beside_it) // (4 - b))):
            beside_it.pop(0)()
        r, s = a[8 * b : 8 * b + 8], e[8 * b : 8 * b + 8]
        d = [[spread(r[p][b], q) for p in range(q + 1)] for q in range(8)]
        m = [[None] * 8 for _ in range(8)]
        inverse = []
        for p in range(8):
            inverse.append(1.0 / d[p][p])
            for q in range(p + 1, 8):
                m[q][p] = d[q][p] * inverse[p]
                for w in range(p + 1, q + 1):
                    d[q][w] = d[q][w] - m[q][p] * d[w][p]
        for p in range(8):
            for q in range(p + 1, 8):
                for jb in range(b + 1, 4):
                    r[q][jb] = r[q][jb] - m[q][p] * r[p][jb]
                for jb in range(b + 1):
                    s[q][jb] = s[q][jb] - m[q][p] * s[p][jb]
        for c in range(b + 1, 4):
            scaled = [r[p][c] * inverse[p] for p in range(8)]
            for i in range(8 * c, 8 * c + 8):
                for p in range(8):
                    k = spread(scaled[p], i % 8)
                    for jb in range(c, 4):
                        a[i][jb] = a[i][jb] - k * r[p][jb]
                    for jb in range(b + 1):
                        e[i][jb] = less(e[i].get(jb), k, s[p][jb])
        for p in range(8):
            scale = lax.rsqrt(d[p][p])
            full = below(*[s[p][jb] * scale for jb in range(b + 1)], *[jnp.zeros((8, SLOTS), F32)] * (3 - b))
            i = 8 * b + p
            result_ref[i * SLOTS : (i + 1) * SLOTS, :] = jnp.transpose(below(full, full, full, full))


def kernel(
    place, near, far, first_factors, mask_hbm, start_hbm, wz0, wz1, wz2, wz3, left, right, dense_hbm, out_hbm,
    dense, updated, left_rows, left_columns, right_rows, inner_rows, gram, gram_parts, right_parts, mixer, mixer_parts,
    raw, square, mix_parts, start, basis, imaged, image_parts, wide_rows, rows, factors, mask, load_sem, out_sem,
):
    tiles, rank, order = left.shape
    r, c = place()
    every = range(tiles)

    def drain(t, half):
        at = pl.ds(half * (order // 2), order // 2)
        return pltpu.make_async_copy(updated.at[t, at], out_hbm.at[t, at], out_sem.at[t, half])

    loads = []
    for q, wz in enumerate((wz0, wz1, wz2, wz3)):
        at = pl.ds(pl.multiple_of((r ^ q) * 128, 128), 128)
        loads.append((wz.at[:, :rank, :], inner_rows.at[:, :, at]))
        loads.append((wz.at[:, rank:, :], right_rows.at[:, rank:, at]))
    loads.append((left, left_rows.at[:, :rank, :]))
    loads.append((right, right_rows.at[:, :rank, :]))
    loads.append((start_hbm, start))
    loads.append((mask_hbm, mask))
    loads.append((dense_hbm, dense))
    loads = [pltpu.make_async_copy(x, y, load_sem.at[i]) for i, (x, y) in enumerate(loads)]
    for copy in loads[:-1]:
        copy.start()

    lanes = lax.broadcasted_iota(jnp.int32, (rank, 128), 1)
    outer, inner = [], []
    for q in range(4):
        even, odd = [
            jnp.where((c ^ p) < 4, near[(c ^ p) % 4].astype(F32), far[(c ^ p) % 4].astype(F32)) for p in (2 * q, 2 * q + 1)
        ]
        outer.append(jnp.where(lanes < 64, even, pltpu.roll(odd, 64, 1)).astype(BF16))
        inner.append(jnp.where(lanes < 64, pltpu.roll(even, 64, 1), odd).astype(BF16))
    outer = beside(*outer)
    inner = beside(*inner)
    for t in every:
        left_rows[t, rank:, :] = outer
    for copy in loads[:-1]:
        copy.wait()
    loads[-1].start()

    row = lax.broadcasted_iota(jnp.int32, (64, 128), 0)
    lane = lax.broadcasted_iota(jnp.int32, (64, 128), 1)
    identity = (lane % 64 == row).astype(F32)
    tail = lane[:rank] % 64 >= rank

    coupling = dot(inner_rows[...].reshape(tiles * rank, order), below(inner, inner, inner, inner), NT)
    for t in every:
        raw[t] = dot(left_rows[t], below(left_rows[t], left_rows[t]), NT)
    for t in every:
        own = -coupling[t * rank : (t + 1) * rank, :]
        mixer[t] = below(identity[:rank], jnp.where(tail, own, 0.0))
        basis[t] = dot(left_32(own), right_32(raw[t, rank:, :]))
    for t in every:
        mixer_parts[t] = right_64(mixer[t])
    for t in every:
        scale = wide_right(mixer[t])
        gram[t] = dot(wide_left(below(raw[t, :rank, :], basis[t])), below(scale, scale), NT) + identity
    for t in every:
        gram_parts[t] = right_64(gram[t])

    def inverse(t):
        return factors[pl.ds(t, rank, SLOTS), :]

    head = start[:, :rank]
    head = left_32(beside(head, head, head, head))
    foot = start[:, rank : 2 * rank]
    foot = left_32(beside(foot, foot, foot, foot))
    for t in every:
        basis[t] = dot(left_32(first_factors[pl.ds(t, rank, SLOTS), :]), right_32(gram[t, :rank, :]))
    for t in every:
        mix_parts[t] = right_32(basis[t])
    for t in every:
        first = mix_parts[t]
        high, middle, low = first[:32], first[32:64], first[128:160]
        square[t] = dot(below(high, high, middle, middle, high, low)[:, :64], first, TN)
    for t in every:
        basis[t] = jnp.where(tail, gram[t, rank:, :] - square[t, rank:, :], 0.0)
        wide_rows[pl.ds(t, rank, SLOTS), :] = basis[t]

    def later(t):
        imaged[t] = dot(head, mix_parts[t])
        right_parts[t] = right_64(dot(right_rows[t], below(right_rows[t], right_rows[t]), NT) + identity)
        left_columns[t] = jnp.transpose(below(left_rows[t], left_rows[t]))

    inverse_factors(wide_rows, factors, rank, [functools.partial(later, t) for t in every])
    for t in every:
        basis[t] = dot(left_32(inverse(t)), right_32(basis[t]))
    for t in every:
        imaged[t] = imaged[t] + dot(foot, right_32(basis[t]))
    for step in range(ITERS):
        for t in every:
            basis[t] = dot(left_64(imaged[t]), right_parts[t])
        for t in every:
            imaged[t] = dot(left_64(basis[t]), gram_parts[t])
        for t in every:
            image_parts[t] = below(*parts3(imaged[t]))
            rows[pl.ds(t, rank, SLOTS), :] = dot(wide_left(imaged[t]), wide_right(basis[t]), NT)
        inverse_factors(rows, factors)
        if step < ITERS - 1:
            for t in every:
                imaged[t] = dot(inverse(t).astype(BF16)[:, :96], image_parts[t])
        else:
            for t in every:
                scale = pick(64, *parts2(inverse(t)))
                high, middle = image_parts[t, :32, :], image_parts[t, 32:64, :]
                imaged[t] = dot(scale, below(high, middle, high, middle))
                high, middle = parts2(basis[t])
                basis[t] = dot(scale, below(high, middle, high, middle))

    loads[-1].wait()
    last = (lane[:rank] % 64 == row[:rank] + rank).astype(F32)
    for t in every:
        square[t, :rank, :] = dot(left_64(basis[t]), mixer_parts[t])
    for t in every:
        admissible = mask[0, t] == 1
        high, low = parts2(jnp.where(admissible, square[t, :rank, :], mixer[t, rank:, :])[:, :64])
        raw[t] = dot(below(high, high, low), paired(jnp.where(admissible, imaged[t], last)), TN)
    for t in every:
        mix_parts[t, :128, :] = below(*parts2(raw[t]))

    def combine(t):
        return dot(left_columns[t], mix_parts[t, :128, :64]).astype(BF16)

    combined = combine(0)
    for t in every:
        admissible = mask[0, t] == 1
        following = combine(t + 1) if t + 1 < tiles else None
        for m in range(0, order, 128):
            added = jnp.where(admissible, 0.0, dense[t, m : m + 128, :].astype(F32))
            updated[t, m : m + 128, :] = (dot(combined[m : m + 128, :], right_rows[t]) + added).astype(BF16)
            if m % (order // 2):
                drain(t, m // (order // 2)).start()
        combined = following
    for t in every:
        drain(t, 0).wait()
        drain(t, 1).wait()


def paired(x):
    high, low = parts2(x)
    return below(high, low, high)


def own_grams(left_hbm, result, left, sem):
    tiles, rank, _ = left.shape
    copy = pltpu.make_async_copy(left_hbm, left, sem)
    copy.start()
    copy.wait()
    row = lax.broadcasted_iota(jnp.int32, (rank, 128), 0)
    lane = lax.broadcasted_iota(jnp.int32, (rank, 128), 1)
    identity = (lane % rank == row).astype(F32)
    for t in range(tiles):
        own = left[t]
        result[pl.ds(t, rank, SLOTS), :] = dot(own, below(own, own, own, own), NT) + identity


LIMIT = pltpu.CompilerParams(vmem_limit_bytes=53964 * 1024)


def local_grams(left):
    vmem = pl.BlockSpec(memory_space=pltpu.VMEM)
    return pl.pallas_call(
        own_grams,
        out_shape=jax.ShapeDtypeStruct((32 * SLOTS, 128), F32),
        in_specs=[pl.BlockSpec(memory_space=pltpu.HBM)],
        out_specs=vmem,
        scratch_shapes=[pltpu.VMEM(left.shape, BF16), pltpu.SemaphoreType.DMA],
        compiler_params=LIMIT,
    )(left)


def local_factors(grams):
    vmem = pl.BlockSpec(memory_space=pltpu.VMEM)
    return pl.pallas_call(
        inverse_factors,
        out_shape=jax.ShapeDtypeStruct((32 * SLOTS, 128), F32),
        in_specs=[vmem],
        out_specs=vmem,
        compiler_params=LIMIT,
    )(grams)


def local_step(place, near, far, first_factors, mask, start, wzs, left, right, dense):
    tiles, rank, order = left.shape
    vmem = pl.BlockSpec(memory_space=pltpu.VMEM)
    hbm = pl.BlockSpec(memory_space=pltpu.HBM)
    free = pl.BlockSpec(memory_space=pl.ANY)
    whole = pltpu.VMEM((tiles, order, order), BF16)
    rows = pltpu.VMEM((tiles, 2 * rank, order), BF16)
    parts = pltpu.VMEM((tiles, 192, 128), BF16)
    square = pltpu.VMEM((tiles, 64, 128), F32)
    small = pltpu.VMEM((tiles, 32, 128), F32)
    return pl.pallas_call(
        functools.partial(kernel, place),
        out_shape=jax.ShapeDtypeStruct(dense.shape, BF16),
        in_specs=[vmem, vmem, vmem, free, free] + [free] * 4 + [hbm] * 3,
        out_specs=hbm,
        scratch_shapes=[
            whole,
            whole,
            rows,
            pltpu.VMEM((tiles, order, 128), BF16),
            rows,
            pltpu.VMEM((tiles, rank, order), BF16),
            square,
            parts,
            parts,
            square,
            parts,
            square,
            square,
            parts,
            pltpu.VMEM((32, 128), F32),
            small,
            small,
            pltpu.VMEM((tiles, 96, 128), BF16),
            pltpu.VMEM((32 * SLOTS, 128), F32),
            pltpu.VMEM((32 * SLOTS, 32), F32),
            pltpu.VMEM((32 * SLOTS, 128), F32),
            pltpu.SMEM((1, tiles), jnp.int32),
            pltpu.SemaphoreType.DMA((13,)),
            pltpu.SemaphoreType.DMA((tiles, 2)),
        ],
        compiler_params=LIMIT,
    )(near, far, first_factors, mask, start, *wzs, left, right, dense)


def turn(x):
    return jnp.swapaxes(x, -1, -2)


def swap(x, axis, size, step):
    return lax.ppermute(x, axis, [(i, i ^ step) for i in range(size)])


def solution(mesh):
    nrow, ncol = mesh.shape["row"], mesh.shape["col"]

    def shards(
        panel_outer, panel_inner, upper_inner, upper_outer, tile_left, tile_right, dense_rows, tile_mask, start_block
    ):
        left, right = turn(tile_left[0]), turn(tile_right[0])
        if nrow == 4 and ncol == 8:
            place = lambda: (lax.axis_index("row"), lax.axis_index("col"))
            pair = jnp.concatenate([turn(panel_outer[0]), turn(panel_inner[0])], -1)
            wz = jnp.concatenate([turn(upper_inner), turn(upper_outer)], 1)
            pair, wz = lax.optimization_barrier((pair, wz))
            near = jnp.stack([pair, swap(pair, "col", 8, 1)])
            wzs = [wz] + [swap(wz, "row", 4, s) for s in (1, 2, 3)]
            near, left_late = lax.optimization_barrier((near, left))
            grams = local_grams(left_late)
            near = jnp.concatenate([near, swap(near, "col", 8, 2)])
            near, grams = lax.optimization_barrier((near, grams))
            far = swap(near, "col", 8, 4)
            first = local_factors(grams)
        else:
            place = lambda: (0, 0)
            wz = jnp.concatenate([turn(upper_inner), turn(upper_outer)], 1)
            both = lax.all_gather(jnp.stack([turn(panel_outer[0]), turn(panel_inner[0])]), "col", axis=2, tiled=True)
            xy = jnp.concatenate([both[0].reshape(32, 8, 64), both[1].reshape(32, 8, 64)], -1).swapaxes(0, 1)
            near, far = xy[:4], xy[4:]
            wz = lax.all_gather(wz, "row", axis=2, tiled=True)
            wzs = [wz[:, :, 128 * q : 128 * q + 128] for q in range(4)]
            first = local_factors(local_grams(left))
        flags = (tile_mask == 1).astype(jnp.int32)
        start = jnp.concatenate([turn(start_block), turn(start_block)], 1)
        updated = local_step(
            place, near, far, first, flags, start, wzs, left, right, dense_rows[0]
        )
        return updated[None]

    placed = (
        P("row", "col", None),
        P("row", "col", None),
        P("col", "row", None),
        P("col", "row", None),
        P("row", "col", None, None),
        P("row", "col", None, None),
        P("row", "col", None, None),
        P("row", "col"),
        P(),
    )
    return jax.shard_map(shards, mesh=mesh, in_specs=placed, out_specs=P("row", "col", None, None), check_vma=False)
```

```python
import functools

import jax
import jax.numpy as jnp
from jax import lax
from jax.experimental import pallas as pl
from jax.experimental.pallas import tpu as pltpu
from jax.sharding import PartitionSpec as P

ITERS = 3
F32, BF16 = jnp.float32, jnp.bfloat16
SLOTS = 16
NN = (((1,), (0,)), ((), ()))
NT = (((1,), (1,)), ((), ()))
TN = (((0,), (0,)), ((), ()))


def dot(a, b, dims=NN):
    return lax.dot_general(a, b, dims, preferred_element_type=F32)


def beside(*parts):
    return jnp.concatenate(parts, axis=1)


def below(*parts):
    return jnp.concatenate(parts, axis=0)


def parts2(x):
    high = x.astype(BF16)
    return high, (x - high.astype(F32)).astype(BF16)


def parts3(x):
    high = x.astype(BF16)
    rest = x - high.astype(F32)
    middle = rest.astype(BF16)
    return high, middle, (rest - middle.astype(F32)).astype(BF16)


def pick(lanes_before, x, y):
    lane = lax.broadcasted_iota(jnp.int32, x.shape, 1)
    return jnp.where(lane < lanes_before, x.astype(F32), y.astype(F32)).astype(BF16)


def left_64(x):
    high, low = parts2(x)
    return beside(high, low[:, :64])


def right_64(x):
    high, low = parts2(x)
    return below(high, low, high)


def left_32(x):
    high, middle, low = parts3(x)
    return beside(pick(64, high, middle), pick(32, high, low)[:, :64])


def right_32(x):
    high, middle, low = parts3(x)
    return below(high, middle, high, middle, low, high)


def wide_left(x):
    high, middle, low = parts3(x)
    return beside(high, middle, pick(64, high, low))


def wide_right(x):
    high, middle, low = parts3(x)
    first = pick(64, high, middle)
    return beside(first, first, pick(64, low, high))


def inverse_factors(rows_ref, result_ref, at=0, beside_it=()):
    sub = lax.broadcasted_iota(jnp.int32, (8, SLOTS), 0)
    one = [(sub == p).astype(F32) for p in range(8)]
    a = []
    for i in range(32):
        turned = jnp.transpose(rows_ref[i * SLOTS : (i + 1) * SLOTS, :])
        a.append({jb: turned[at + jb * 8 : at + jb * 8 + 8, :] for jb in range(i // 8, 4)})
    e = [{i // 8: one[i % 8]} for i in range(32)]

    def spread(x, p):
        return jnp.broadcast_to(x[p : p + 1, :], (8, SLOTS))

    def less(x, m, y):
        return -(m * y) if x is None else x - m * y

    beside_it = list(beside_it)
    for b in range(4):
        for _ in range(-(-len(beside_it) // (4 - b))):
            beside_it.pop(0)()
        r, s = a[8 * b : 8 * b + 8], e[8 * b : 8 * b + 8]
        d = [[spread(r[p][b], q) for p in range(q + 1)] for q in range(8)]
        m = [[None] * 8 for _ in range(8)]
        inverse = []
        for p in range(8):
            inverse.append(1.0 / d[p][p])
            for q in range(p + 1, 8):
                m[q][p] = d[q][p] * inverse[p]
                for w in range(p + 1, q + 1):
                    d[q][w] = d[q][w] - m[q][p] * d[w][p]
        for p in range(8):
            for q in range(p + 1, 8):
                for jb in range(b + 1, 4):
                    r[q][jb] = r[q][jb] - m[q][p] * r[p][jb]
                for jb in range(b + 1):
                    s[q][jb] = s[q][jb] - m[q][p] * s[p][jb]
        for c in range(b + 1, 4):
            scaled = [r[p][c] * inverse[p] for p in range(8)]
            for i in range(8 * c, 8 * c + 8):
                for p in range(8):
                    k = spread(scaled[p], i % 8)
                    for jb in range(c, 4):
                        a[i][jb] = a[i][jb] - k * r[p][jb]
                    for jb in range(b + 1):
                        e[i][jb] = less(e[i].get(jb), k, s[p][jb])
        for p in range(8):
            scale = lax.rsqrt(d[p][p])
            full = below(*[s[p][jb] * scale for jb in range(b + 1)], *[jnp.zeros((8, SLOTS), F32)] * (3 - b))
            i = 8 * b + p
            result_ref[i * SLOTS : (i + 1) * SLOTS, :] = jnp.transpose(below(full, full, full, full))


def kernel(
    place, near, far, first_factors, flags, start, wz0, wz1, wz2, wz3, left, right, dense_hbm, out_hbm,
    dense, updated, left_rows, left_columns, right_rows, gram, gram_parts, right_parts, mixer, mixer_parts,
    raw, square, mix_parts, basis, imaged, image_parts, wide_rows, rows, factors, mask, load_sem, out_sem,
):
    tiles, rank, order = left.shape
    r, c = place()
    every = range(tiles)

    def drain(t, half):
        at = pl.ds(half * (order // 2), order // 2)
        return pltpu.make_async_copy(updated.at[t, at], out_hbm.at[t, at], out_sem.at[t, half])

    loads = [(left, left_rows.at[:, :rank, :]), (right, right_rows.at[:, :rank, :]), (flags, mask)]
    for q, wz in enumerate((wz0, wz1, wz2, wz3)):
        at = pl.ds(pl.multiple_of((r ^ q) * 128, 128), 128)
        loads.append((wz.at[:, rank:, :], right_rows.at[:, rank:, at]))
    loads.append((dense_hbm, dense))
    loads = [pltpu.make_async_copy(x, y, load_sem.at[i]) for i, (x, y) in enumerate(loads)]
    for copy in loads[:-1]:
        copy.start()

    lanes = lax.broadcasted_iota(jnp.int32, (rank, 128), 1)

    def blocks(q):
        found = []
        for p in (c ^ (2 * q), c ^ (2 * q + 1)):
            found.append(jnp.where(p < 4, near[p % 4].astype(F32), far[p % 4].astype(F32)))
        return found

    coupling = 0.0
    for q, wz in enumerate((wz0, wz1, wz2, wz3)):
        even, odd = blocks(r ^ q)
        inner = jnp.where(lanes < 64, pltpu.roll(even, 64, 1), odd).astype(BF16)
        coupling += dot(wz[:, :rank, :].reshape(tiles * rank, 128), below(inner, inner, inner, inner), NT)
    outer = []
    for q in range(4):
        even, odd = blocks(q)
        outer.append(jnp.where(lanes < 64, even, pltpu.roll(odd, 64, 1)).astype(BF16))
    outer = beside(*outer)
    for t in every:
        left_rows[t, rank:, :] = outer
    loads[0].wait()
    row = lax.broadcasted_iota(jnp.int32, (64, 128), 0)
    lane = lax.broadcasted_iota(jnp.int32, (64, 128), 1)
    identity = (lane % 64 == row).astype(F32)
    tail = lane[:rank] % 64 >= rank

    for t in every:
        raw[t] = dot(left_rows[t], below(left_rows[t], left_rows[t]), NT)
    for t in every:
        own = -coupling[t * rank : (t + 1) * rank, :]
        mixer[t] = below(identity[:rank], jnp.where(tail, own, 0.0))
        basis[t] = dot(left_32(own), right_32(raw[t, rank:, :]))
    for t in every:
        mixer_parts[t] = right_64(mixer[t])
    for t in every:
        scale = wide_right(mixer[t])
        gram[t] = dot(wide_left(below(raw[t, :rank, :], basis[t])), below(scale, scale), NT) + identity
    for t in every:
        gram_parts[t] = right_64(gram[t])

    for copy in loads[1:-1]:
        copy.wait()
    loads[-1].start()

    def inverse(t):
        return factors[pl.ds(t, rank, SLOTS), :]

    head = start[:, :rank]
    head = left_32(beside(head, head, head, head))
    foot = start[:, rank : 2 * rank]
    foot = left_32(beside(foot, foot, foot, foot))
    for t in every:
        basis[t] = dot(left_32(first_factors[pl.ds(t, rank, SLOTS), :]), right_32(gram[t, :rank, :]))
    for t in every:
        mix_parts[t] = right_32(basis[t])
    for t in every:
        first = mix_parts[t]
        high, middle, low = first[:32], first[32:64], first[128:160]
        square[t] = dot(below(high, high, middle, middle, high, low)[:, :64], first, TN)
    for t in every:
        basis[t] = jnp.where(tail, gram[t, rank:, :] - square[t, rank:, :], 0.0)
        wide_rows[pl.ds(t, rank, SLOTS), :] = basis[t]

    def later(t):
        imaged[t] = dot(head, mix_parts[t])
        right_parts[t] = right_64(dot(right_rows[t], below(right_rows[t], right_rows[t]), NT) + identity)
        left_columns[t] = jnp.transpose(below(left_rows[t], left_rows[t]))

    inverse_factors(wide_rows, factors, rank, [functools.partial(later, t) for t in every])
    for t in every:
        basis[t] = dot(left_32(inverse(t)), right_32(basis[t]))
    for t in every:
        imaged[t] = imaged[t] + dot(foot, right_32(basis[t]))
    for step in range(ITERS):
        for t in every:
            basis[t] = dot(left_64(imaged[t]), right_parts[t])
        for t in every:
            imaged[t] = dot(left_64(basis[t]), gram_parts[t])
        for t in every:
            high, middle, low = parts3(imaged[t])
            image_parts[t] = below(high, middle, low)
            rows[pl.ds(t, rank, SLOTS), :] = dot(
                beside(high, middle, pick(64, high, low)), wide_right(basis[t]), NT
            )
        if step < ITERS - 1:
            inverse_factors(rows, factors)
            for t in every:
                imaged[t] = dot(inverse(t).astype(BF16)[:, :96], image_parts[t])

    def spread(t):
        basis[t] = dot(left_64(basis[t]), mixer_parts[t])

    inverse_factors(rows, factors, 0, [functools.partial(spread, t) for t in every])
    for t in every:
        scale = pick(64, *parts2(inverse(t)))
        high, middle = image_parts[t, :32, :], image_parts[t, 32:64, :]
        imaged[t] = dot(scale, below(high, middle, high, middle))
        high, middle = parts2(basis[t])
        basis[t] = dot(scale, below(high, middle, high, middle))

    loads[-1].wait()
    last = (lane[:rank] % 64 == row[:rank] + rank).astype(F32)
    for t in every:
        admissible = mask[0, t] == 1
        high, low = parts2(jnp.where(admissible, basis[t], mixer[t, rank:, :])[:, :64])
        raw[t] = dot(below(high, high, low), paired(jnp.where(admissible, imaged[t], last)), TN)
    for t in every:
        mix_parts[t, :128, :] = below(*parts2(raw[t]))

    def combine(t):
        return dot(left_columns[t], mix_parts[t, :128, :64]).astype(BF16)

    combined = combine(0)
    for t in every:
        admissible = mask[0, t] == 1
        following = combine(t + 1) if t + 1 < tiles else None
        for m in range(0, order, 128):
            added = jnp.where(admissible, 0.0, dense[t, m : m + 128, :].astype(F32))
            updated[t, m : m + 128, :] = (dot(combined[m : m + 128, :], right_rows[t]) + added).astype(BF16)
            if m % (order // 2):
                drain(t, m // (order // 2)).start()
        combined = following
    for t in every:
        drain(t, 0).wait()
        drain(t, 1).wait()


def paired(x):
    high, low = parts2(x)
    return below(high, low, high)


def own_grams(left, result):
    tiles, rank, _ = left.shape
    row = lax.broadcasted_iota(jnp.int32, (rank, 128), 0)
    lane = lax.broadcasted_iota(jnp.int32, (rank, 128), 1)
    identity = (lane % rank == row).astype(F32)
    for t in range(tiles):
        own = left[t]
        result[pl.ds(t, rank, SLOTS), :] = dot(own, below(own, own, own, own), NT) + identity


LIMIT = pltpu.CompilerParams(vmem_limit_bytes=54000 * 1024)


def local_grams(left):
    vmem = pl.BlockSpec(memory_space=pltpu.VMEM)
    return pl.pallas_call(
        own_grams,
        out_shape=jax.ShapeDtypeStruct((32 * SLOTS, 128), F32),
        in_specs=[vmem],
        out_specs=vmem,
        compiler_params=LIMIT,
    )(left)


def local_factors(grams):
    vmem = pl.BlockSpec(memory_space=pltpu.VMEM)
    return pl.pallas_call(
        inverse_factors,
        out_shape=jax.ShapeDtypeStruct((32 * SLOTS, 128), F32),
        in_specs=[vmem],
        out_specs=vmem,
        compiler_params=LIMIT,
    )(grams)


def local_step(place, near, far, first_factors, flags, start, wzs, left, right, dense):
    tiles, rank, order = left.shape
    vmem = pl.BlockSpec(memory_space=pltpu.VMEM)
    hbm = pl.BlockSpec(memory_space=pltpu.HBM)
    free = pl.BlockSpec(memory_space=pl.ANY)
    whole = pltpu.VMEM((tiles, order, order), BF16)
    rows = pltpu.VMEM((tiles, 2 * rank, order), BF16)
    parts = pltpu.VMEM((tiles, 192, 128), BF16)
    square = pltpu.VMEM((tiles, 64, 128), F32)
    small = pltpu.VMEM((tiles, 32, 128), F32)
    return pl.pallas_call(
        functools.partial(kernel, place),
        out_shape=jax.ShapeDtypeStruct(dense.shape, BF16),
        in_specs=[vmem] * 3 + [free] + [vmem] * 5 + [hbm] * 3,
        out_specs=hbm,
        scratch_shapes=[
            whole,
            whole,
            rows,
            pltpu.VMEM((tiles, order, 128), BF16),
            rows,
            square,
            parts,
            parts,
            square,
            parts,
            square,
            square,
            parts,
            small,
            small,
            pltpu.VMEM((tiles, 96, 128), BF16),
            pltpu.VMEM((32 * SLOTS, 128), F32),
            pltpu.VMEM((32 * SLOTS, 32), F32),
            pltpu.VMEM((32 * SLOTS, 128), F32),
            pltpu.SMEM((1, tiles), jnp.int32),
            pltpu.SemaphoreType.DMA((8,)),
            pltpu.SemaphoreType.DMA((tiles, 2)),
        ],
        compiler_params=LIMIT,
    )(near, far, first_factors, flags, start, *wzs, left, right, dense)


def turn(x):
    return jnp.swapaxes(x, -1, -2)


def swap(x, axis, size, step):
    return lax.ppermute(x, axis, [(i, i ^ step) for i in range(size)])


def solution(mesh):
    nrow, ncol = mesh.shape["row"], mesh.shape["col"]

    def shards(
        panel_outer, panel_inner, upper_inner, upper_outer, tile_left, tile_right, dense_rows, tile_mask, start_block
    ):
        left, right = turn(tile_left[0]), turn(tile_right[0])
        if nrow == 4 and ncol == 8:
            place = lambda: (lax.axis_index("row"), lax.axis_index("col"))
            pair = jnp.concatenate([turn(panel_outer[0]), turn(panel_inner[0])], -1)
            wz = jnp.concatenate([turn(upper_inner), turn(upper_outer)], 1)
            pair, wz = lax.optimization_barrier((pair, wz))
            near = jnp.stack([pair, swap(pair, "col", 8, 1)])
            wzs = [wz] + [swap(wz, "row", 4, s) for s in (1, 2, 3)]
            near, left_late = lax.optimization_barrier((near, left))
            grams = local_grams(left_late)
            near = jnp.concatenate([near, swap(near, "col", 8, 2)])
            near, grams = lax.optimization_barrier((near, grams))
            far = swap(near, "col", 8, 4)
            first = local_factors(grams)
        else:
            place = lambda: (0, 0)
            wz = jnp.concatenate([turn(upper_inner), turn(upper_outer)], 1)
            both = lax.all_gather(jnp.stack([turn(panel_outer[0]), turn(panel_inner[0])]), "col", axis=2, tiled=True)
            xy = jnp.concatenate([both[0].reshape(32, 8, 64), both[1].reshape(32, 8, 64)], -1).swapaxes(0, 1)
            near, far = xy[:4], xy[4:]
            wz = lax.all_gather(wz, "row", axis=2, tiled=True)
            wzs = [wz[:, :, 128 * q : 128 * q + 128] for q in range(4)]
            first = local_factors(local_grams(left))
        flags = (tile_mask == 1).astype(jnp.int32)
        start = jnp.concatenate([turn(start_block), turn(start_block)], 1)
        updated = local_step(
            place, near, far, first, flags, start, wzs, left, right, dense_rows[0]
        )
        return updated[None]

    placed = (
        P("row", "col", None),
        P("row", "col", None),
        P("col", "row", None),
        P("col", "row", None),
        P("row", "col", None, None),
        P("row", "col", None, None),
        P("row", "col", None, None),
        P("row", "col"),
        P(),
    )
    return jax.shard_map(shards, mesh=mesh, in_specs=placed, out_specs=P("row", "col", None, None), check_vma=False)
```

```python
import functools

import jax
import jax.numpy as jnp
from jax import lax
from jax.experimental import pallas as pl
from jax.experimental.pallas import tpu as pltpu
from jax.sharding import PartitionSpec as P

ITERS = 3
F32, BF16 = jnp.float32, jnp.bfloat16
SLOTS = 16
NN = (((1,), (0,)), ((), ()))
NT = (((1,), (1,)), ((), ()))
TN = (((0,), (0,)), ((), ()))


def dot(a, b, dims=NN):
    return lax.dot_general(a, b, dims, preferred_element_type=F32)


def beside(*parts):
    return jnp.concatenate(parts, axis=1)


def below(*parts):
    return jnp.concatenate(parts, axis=0)


def parts2(x):
    high = x.astype(BF16)
    return high, (x - high.astype(F32)).astype(BF16)


def parts3(x):
    high = x.astype(BF16)
    rest = x - high.astype(F32)
    middle = rest.astype(BF16)
    return high, middle, (rest - middle.astype(F32)).astype(BF16)


def pick(lanes_before, x, y):
    lane = lax.broadcasted_iota(jnp.int32, x.shape, 1)
    return jnp.where(lane < lanes_before, x.astype(F32), y.astype(F32)).astype(BF16)


def left_64(x):
    high, low = parts2(x)
    return beside(high, low[:, :64])


def right_64(x):
    high, low = parts2(x)
    return below(high, low, high)


def left_32(x):
    high, middle, low = parts3(x)
    return beside(pick(64, high, middle), pick(32, high, low)[:, :64])


def right_32(x):
    high, middle, low = parts3(x)
    return below(high, middle, high, middle, low, high)


def wide_left(x):
    high, middle, low = parts3(x)
    return beside(high, middle, pick(64, high, low))


def wide_right(x):
    high, middle, low = parts3(x)
    first = pick(64, high, middle)
    return beside(first, first, pick(64, low, high))


def inverse_factors(rows_ref, result_ref, at=0, beside_it=()):
    sub = lax.broadcasted_iota(jnp.int32, (8, SLOTS), 0)
    one = [(sub == p).astype(F32) for p in range(8)]
    a = []
    for i in range(32):
        turned = jnp.transpose(rows_ref[i * SLOTS : (i + 1) * SLOTS, :])
        a.append({jb: turned[at + jb * 8 : at + jb * 8 + 8, :] for jb in range(i // 8, 4)})
    e = [{i // 8: one[i % 8]} for i in range(32)]

    def spread(x, p):
        return jnp.broadcast_to(x[p : p + 1, :], (8, SLOTS))

    def less(x, m, y):
        return -(m * y) if x is None else x - m * y

    beside_it = list(beside_it)
    for b in range(4):
        for _ in range(-(-len(beside_it) // (4 - b))):
            beside_it.pop(0)()
        r, s = a[8 * b : 8 * b + 8], e[8 * b : 8 * b + 8]
        d = [[spread(r[p][b], q) for p in range(q + 1)] for q in range(8)]
        m = [[None] * 8 for _ in range(8)]
        inverse = []
        for p in range(8):
            inverse.append(1.0 / d[p][p])
            for q in range(p + 1, 8):
                m[q][p] = d[q][p] * inverse[p]
                for w in range(p + 1, q + 1):
                    d[q][w] = d[q][w] - m[q][p] * d[w][p]
        for p in range(8):
            for q in range(p + 1, 8):
                for jb in range(b + 1, 4):
                    r[q][jb] = r[q][jb] - m[q][p] * r[p][jb]
                for jb in range(b + 1):
                    s[q][jb] = s[q][jb] - m[q][p] * s[p][jb]
        for c in range(b + 1, 4):
            scaled = [r[p][c] * inverse[p] for p in range(8)]
            for i in range(8 * c, 8 * c + 8):
                for p in range(8):
                    k = spread(scaled[p], i % 8)
                    for jb in range(c, 4):
                        a[i][jb] = a[i][jb] - k * r[p][jb]
                    for jb in range(b + 1):
                        e[i][jb] = less(e[i].get(jb), k, s[p][jb])
        for p in range(8):
            scale = lax.rsqrt(d[p][p])
            full = below(*[s[p][jb] * scale for jb in range(b + 1)], *[jnp.zeros((8, SLOTS), F32)] * (3 - b))
            i = 8 * b + p
            result_ref[i * SLOTS : (i + 1) * SLOTS, :] = jnp.transpose(below(full, full, full, full))


def kernel(
    place, near, far, first_factors, flags, start, wz0, wz1, wz2, wz3, left, right, dense_hbm, out_hbm,
    dense, updated, left_rows, left_columns, right_rows, gram, gram_parts, right_parts, mixer, mixer_parts,
    raw, square, mix_parts, basis, imaged, image_parts, wide_rows, rows, factors, mask, load_sem, out_sem,
):
    tiles, rank, order = left.shape
    r, c = place()
    every = range(tiles)

    def drain(t, half):
        at = pl.ds(half * (order // 2), order // 2)
        return pltpu.make_async_copy(updated.at[t, at], out_hbm.at[t, at], out_sem.at[t, half])

    loads = [(left, left_rows.at[:, :rank, :]), (right, right_rows.at[:, :rank, :]), (flags, mask)]
    for q, wz in enumerate((wz0, wz1, wz2, wz3)):
        at = pl.ds(pl.multiple_of((r ^ q) * 128, 128), 128)
        loads.append((wz.at[:, rank:, :], right_rows.at[:, rank:, at]))
    loads.append((dense_hbm, dense))
    loads = [pltpu.make_async_copy(x, y, load_sem.at[i]) for i, (x, y) in enumerate(loads)]
    for copy in loads[:-1]:
        copy.start()

    lanes = lax.broadcasted_iota(jnp.int32, (rank, 128), 1)

    def blocks(q):
        found = []
        for p in (c ^ (2 * q), c ^ (2 * q + 1)):
            found.append(jnp.where(p < 4, near[p % 4].astype(F32), far[p % 4].astype(F32)))
        return found

    coupling = 0.0
    for q, wz in enumerate((wz0, wz1, wz2, wz3)):
        even, odd = blocks(r ^ q)
        inner = jnp.where(lanes < 64, pltpu.roll(even, 64, 1), odd).astype(BF16)
        coupling += dot(wz[:, :rank, :].reshape(tiles * rank, 128), below(inner, inner, inner, inner), NT)
    outer = []
    for q in range(4):
        even, odd = blocks(q)
        outer.append(jnp.where(lanes < 64, even, pltpu.roll(odd, 64, 1)).astype(BF16))
    outer = beside(*outer)
    for t in every:
        left_rows[t, rank:, :] = outer
    loads[0].wait()
    row = lax.broadcasted_iota(jnp.int32, (64, 128), 0)
    lane = lax.broadcasted_iota(jnp.int32, (64, 128), 1)
    identity = (lane % 64 == row).astype(F32)
    tail = lane[:rank] % 64 >= rank

    for t in every:
        raw[t] = dot(left_rows[t], below(left_rows[t], left_rows[t]), NT)
    for t in every:
        own = -coupling[t * rank : (t + 1) * rank, :]
        mixer[t] = below(identity[:rank], jnp.where(tail, own, 0.0))
        basis[t] = dot(left_32(own), right_32(raw[t, rank:, :]))
    for t in every:
        mixer_parts[t] = right_64(mixer[t])
    for t in every:
        scale = wide_right(mixer[t])
        gram[t] = dot(wide_left(below(raw[t, :rank, :], basis[t])), below(scale, scale), NT) + identity
    for t in every:
        gram_parts[t] = right_64(gram[t])

    for copy in loads[1:-1]:
        copy.wait()
    loads[-1].start()

    def inverse(t):
        return factors[pl.ds(t, rank, SLOTS), :]

    head = start[:, :rank]
    head = left_32(beside(head, head, head, head))
    foot = start[:, rank : 2 * rank]
    foot = left_32(beside(foot, foot, foot, foot))
    for t in every:
        basis[t] = dot(left_32(first_factors[pl.ds(t, rank, SLOTS), :]), right_32(gram[t, :rank, :]))
    for t in every:
        mix_parts[t] = right_32(basis[t])
    for t in every:
        first = mix_parts[t]
        high, middle, low = first[:32], first[32:64], first[128:160]
        square[t] = dot(below(high, high, middle, middle, high, low)[:, :64], first, TN)
    for t in every:
        basis[t] = jnp.where(tail, gram[t, rank:, :] - square[t, rank:, :], 0.0)
        wide_rows[pl.ds(t, rank, SLOTS), :] = basis[t]

    def later(t):
        imaged[t] = dot(head, mix_parts[t])
        right_parts[t] = right_64(dot(right_rows[t], below(right_rows[t], right_rows[t]), NT) + identity)

    def turned(t):
        left_columns[t] = jnp.transpose(below(left_rows[t], left_rows[t]))

    inverse_factors(wide_rows, factors, rank, [functools.partial(later, t) for t in every])
    for t in every:
        basis[t] = dot(left_32(inverse(t)), right_32(basis[t]))
    for t in every:
        imaged[t] = imaged[t] + dot(foot, right_32(basis[t]))
    for step in range(ITERS):
        for t in every:
            basis[t] = dot(left_64(imaged[t]), right_parts[t])
        for t in every:
            imaged[t] = dot(left_64(basis[t]), gram_parts[t])
        for t in every:
            high, middle, low = parts3(imaged[t])
            image_parts[t] = below(high, middle, low)
            rows[pl.ds(t, rank, SLOTS), :] = dot(
                beside(high, middle, pick(64, high, low)), wide_right(basis[t]), NT
            )
        if step < ITERS - 1:
            inverse_factors(rows, factors, 0, [functools.partial(turned, t) for t in every[step * 6 : step * 6 + 6]])
            for t in every:
                imaged[t] = dot(inverse(t).astype(BF16)[:, :96], image_parts[t])

    def spread(t):
        basis[t] = dot(left_64(basis[t]), mixer_parts[t])

    inverse_factors(rows, factors, 0, [functools.partial(spread, t) for t in every])
    for t in every:
        scale = pick(64, *parts2(inverse(t)))
        high, middle = image_parts[t, :32, :], image_parts[t, 32:64, :]
        imaged[t] = dot(scale, below(high, middle, high, middle))
        high, middle = parts2(basis[t])
        basis[t] = dot(scale, below(high, middle, high, middle))

    loads[-1].wait()
    last = (lane[:rank] % 64 == row[:rank] + rank).astype(F32)
    for t in every:
        admissible = mask[0, t] == 1
        high, low = parts2(jnp.where(admissible, basis[t], mixer[t, rank:, :])[:, :64])
        raw[t] = dot(below(high, high, low), paired(jnp.where(admissible, imaged[t], last)), TN)
    for t in every:
        mix_parts[t, :128, :] = below(*parts2(raw[t]))

    def combine(t):
        return dot(left_columns[t], mix_parts[t, :128, :64]).astype(BF16)

    combined = combine(0)
    for t in every:
        admissible = mask[0, t] == 1
        following = combine(t + 1) if t + 1 < tiles else None
        for m in range(0, order, 128):
            added = jnp.where(admissible, 0.0, dense[t, m : m + 128, :].astype(F32))
            updated[t, m : m + 128, :] = (dot(combined[m : m + 128, :], right_rows[t]) + added).astype(BF16)
            if m % (order // 2):
                drain(t, m // (order // 2)).start()
        combined = following
    for t in every:
        drain(t, 0).wait()
        drain(t, 1).wait()


def paired(x):
    high, low = parts2(x)
    return below(high, low, high)


def own_grams(left, result):
    tiles, rank, _ = left.shape
    row = lax.broadcasted_iota(jnp.int32, (rank, 128), 0)
    lane = lax.broadcasted_iota(jnp.int32, (rank, 128), 1)
    identity = (lane % rank == row).astype(F32)
    for t in range(tiles):
        own = left[t]
        result[pl.ds(t, rank, SLOTS), :] = dot(own, below(own, own, own, own), NT) + identity


LIMIT = pltpu.CompilerParams(vmem_limit_bytes=54000 * 1024)


def local_grams(left):
    vmem = pl.BlockSpec(memory_space=pltpu.VMEM)
    return pl.pallas_call(
        own_grams,
        out_shape=jax.ShapeDtypeStruct((32 * SLOTS, 128), F32),
        in_specs=[vmem],
        out_specs=vmem,
        compiler_params=LIMIT,
    )(left)


def local_factors(grams):
    vmem = pl.BlockSpec(memory_space=pltpu.VMEM)
    return pl.pallas_call(
        inverse_factors,
        out_shape=jax.ShapeDtypeStruct((32 * SLOTS, 128), F32),
        in_specs=[vmem],
        out_specs=vmem,
        compiler_params=LIMIT,
    )(grams)


def local_step(place, near, far, first_factors, flags, start, wzs, left, right, dense):
    tiles, rank, order = left.shape
    vmem = pl.BlockSpec(memory_space=pltpu.VMEM)
    hbm = pl.BlockSpec(memory_space=pltpu.HBM)
    free = pl.BlockSpec(memory_space=pl.ANY)
    whole = pltpu.VMEM((tiles, order, order), BF16)
    rows = pltpu.VMEM((tiles, 2 * rank, order), BF16)
    parts = pltpu.VMEM((tiles, 192, 128), BF16)
    square = pltpu.VMEM((tiles, 64, 128), F32)
    small = pltpu.VMEM((tiles, 32, 128), F32)
    return pl.pallas_call(
        functools.partial(kernel, place),
        out_shape=jax.ShapeDtypeStruct(dense.shape, BF16),
        in_specs=[vmem] * 3 + [free] + [vmem] * 5 + [hbm] * 3,
        out_specs=hbm,
        scratch_shapes=[
            whole,
            whole,
            rows,
            pltpu.VMEM((tiles, order, 128), BF16),
            rows,
            square,
            parts,
            parts,
            square,
            parts,
            square,
            square,
            parts,
            small,
            small,
            pltpu.VMEM((tiles, 96, 128), BF16),
            pltpu.VMEM((32 * SLOTS, 128), F32),
            pltpu.VMEM((32 * SLOTS, 32), F32),
            pltpu.VMEM((32 * SLOTS, 128), F32),
            pltpu.SMEM((1, tiles), jnp.int32),
            pltpu.SemaphoreType.DMA((8,)),
            pltpu.SemaphoreType.DMA((tiles, 2)),
        ],
        compiler_params=LIMIT,
    )(near, far, first_factors, flags, start, *wzs, left, right, dense)


def turn(x):
    return jnp.swapaxes(x, -1, -2)


def swap(x, axis, size, step):
    return lax.ppermute(x, axis, [(i, i ^ step) for i in range(size)])


def solution(mesh):
    nrow, ncol = mesh.shape["row"], mesh.shape["col"]

    def shards(
        panel_outer, panel_inner, upper_inner, upper_outer, tile_left, tile_right, dense_rows, tile_mask, start_block
    ):
        left, right = turn(tile_left[0]), turn(tile_right[0])
        if nrow == 4 and ncol == 8:
            place = lambda: (lax.axis_index("row"), lax.axis_index("col"))
            pair = jnp.concatenate([turn(panel_outer[0]), turn(panel_inner[0])], -1)
            wz = jnp.concatenate([turn(upper_inner), turn(upper_outer)], 1)
            pair, wz = lax.optimization_barrier((pair, wz))
            near = jnp.stack([pair, swap(pair, "col", 8, 1)])
            wzs = [wz] + [swap(wz, "row", 4, s) for s in (1, 2, 3)]
            near, left_late = lax.optimization_barrier((near, left))
            grams = local_grams(left_late)
            near = jnp.concatenate([near, swap(near, "col", 8, 2)])
            near, grams = lax.optimization_barrier((near, grams))
            far = swap(near, "col", 8, 4)
            first = local_factors(grams)
        else:
            place = lambda: (0, 0)
            wz = jnp.concatenate([turn(upper_inner), turn(upper_outer)], 1)
            both = lax.all_gather(jnp.stack([turn(panel_outer[0]), turn(panel_inner[0])]), "col", axis=2, tiled=True)
            xy = jnp.concatenate([both[0].reshape(32, 8, 64), both[1].reshape(32, 8, 64)], -1).swapaxes(0, 1)
            near, far = xy[:4], xy[4:]
            wz = lax.all_gather(wz, "row", axis=2, tiled=True)
            wzs = [wz[:, :, 128 * q : 128 * q + 128] for q in range(4)]
            first = local_factors(local_grams(left))
        flags = (tile_mask == 1).astype(jnp.int32)
        start = jnp.concatenate([turn(start_block), turn(start_block)], 1)
        updated = local_step(
            place, near, far, first, flags, start, wzs, left, right, dense_rows[0]
        )
        return updated[None]

    placed = (
        P("row", "col", None),
        P("row", "col", None),
        P("col", "row", None),
        P("col", "row", None),
        P("row", "col", None, None),
        P("row", "col", None, None),
        P("row", "col", None, None),
        P("row", "col"),
        P(),
    )
    return jax.shard_map(shards, mesh=mesh, in_specs=placed, out_specs=P("row", "col", None, None), check_vma=False)
```
